128 devices in a mesh: dp: 64 (over y, x, z_hi, core), mp: 2 (over z_lo).
Axes of the slice: x: 4, y: 4, z: 4 (z_hi: 2, z_lo: 2; z = z_hi * 2 + z_lo), core: 2. Of those that a mesh axis runs over, the one named last changes fastest.
Arguments:
- doc_states: bfloat16 [262144, 1024], P('dp'), may hold values from -6 to 6
- phrase_start: int32 [65536], P('dp'), may hold values from 0 to 4095
- phrase_span: int32 [65536], P('dp'), may hold values from 0 to 8
- start_in: bfloat16 [1024, 1024], P(None, 'mp'), may hold values from -0.1875 to 0.1875
- start_out: bfloat16 [1024, 512], P('mp'), may hold values from -0.1875 to 0.1875
- end_in: bfloat16 [1024, 1024], P(None, 'mp'), may hold values from -0.1875 to 0.1875
- end_out: bfloat16 [1024, 512], P('mp'), may hold values from -0.1875 to 0.1875
- token_table: bfloat16 [32768, 1024], P(('dp', 'mp')), may hold values from -8 to 8
- queries: bfloat16 [16384, 1024], P(('dp', 'mp')), may hold values from -32 to 32
- targets: int32 [16384], P(('dp', 'mp')), may hold values from 0 to 98303
Outputs:
- losses: float32 [16384], P(('dp', 'mp'))
The draws below stay inside these ranges and needn't reach their ends.
All inputs are finite; a program needn't handle non-finite values.
Results may differ from the reference program's by a relative error of at most 0.0003.
Values may be sent and summed in bfloat16 or wider, within the bound.
No kernel may reach another device: no remote copies, remote signals or barrier semaphores. Data moves between devices by JAX's collectives and lax.ppermute only.
A program may use at most 192 MiB of HBM per device.

```python
import math
import jax
import jax.numpy as jnp
from jax import lax

H = 1024
FFN = 1024
V = 32768
PH_DP = 1024
MAX_SPAN = 8
HALF = 512
DOC_DEV = 4096
DOCS = 262144
PHRASES = 65536
QUERIES = 16384


def table_draw(key, spread):
    base = jax.random.normal(key, (V, H), jnp.float32)
    noise = jax.random.normal(jax.random.fold_in(key, 11), (V, H), jnp.float32)
    leading = base[0::2]
    second = noise[1::2]
    pair_scale = jnp.exp(jax.random.uniform(jax.random.fold_in(key, 12), (V // 2, 1), jnp.float32, -spread, spread))
    stacked = jnp.stack([leading * pair_scale, second * pair_scale], axis=1).reshape(V, H)
    return jnp.clip(stacked, -8.0, 8.0)


def query_values(key, table):
    own_key = jax.random.fold_in(key, 5)
    key_one = jax.random.fold_in(own_key, 0)
    key_three = jax.random.fold_in(own_key, 2)
    key_four = jax.random.fold_in(own_key, 3)
    drawn = jax.random.normal(key_one, (QUERIES, H), jnp.float32)
    leading = jax.random.randint(key_three, (QUERIES,), 0, V // 2) * 2
    strength = jax.random.uniform(key_four, (QUERIES, 1), jnp.float32, 70.0, 200.0) / math.sqrt(H)
    aligned = strength * (table[leading] + table[leading + 1]) * 0.5
    chosen = (jnp.arange(QUERIES) % 37 == 0)[:, None]
    values = jnp.where(chosen, aligned, drawn)
    return jnp.clip(values, -32.0, 32.0)


def draw_token_table(key, part):
    table = table_draw(key, 0.0)
    return table.astype(jnp.bfloat16)


def draw_queries(key, part):
    values = query_values(key, table_draw(key, 0.0))
    return values.astype(jnp.bfloat16)


def touch_ends(entries, rng, least, high):
    spot = [jax.random.randint(jax.random.fold_in(rng, axis), (), 0, length) for axis, length in enumerate(entries.shape)]
    main_axis = entries.shape.index(max(entries.shape))
    neighbour = spot[:main_axis] + [(spot[main_axis] + 1) % entries.shape[main_axis]] + spot[main_axis + 1:]
    return entries.at[tuple(spot)].set(least).at[tuple(neighbour)].set(high)


def block_scale(key, extent, cuts, least, top_value):
    level, own = 1.0, jax.random.fold_in(key, 6)
    for position, blocks in cuts:
        heights = jnp.exp(jax.random.uniform(jax.random.fold_in(own, position), (blocks,), jnp.float32, least / len(cuts), top_value / len(cuts)))
        level = level * jnp.repeat(heights, extent[position] // blocks).reshape([-1 if axis == position else 1 for axis in range(len(extent))])
    return level


def scatter_about(rng, dims, scale, reach, cuts=(), kind=jnp.bfloat16):
    entries = scale * jax.random.normal(rng, dims, jnp.float32)
    if cuts:
        entries = entries * block_scale(rng, dims, cuts, -0.22, 0.18)
    return jnp.clip(entries, -reach, reach).astype(kind)


def setup_inputs(seed: int = 0) -> dict:
    arg_keys = jax.random.split(jax.random.key(seed), 11)
    return {
        "doc_states": scatter_about(arg_keys[0], (DOCS, H), 1.0, 6.0, ((0, 64),)),
        "phrase_start": touch_ends(jax.random.randint(arg_keys[1], (PHRASES,), 0, DOC_DEV), jax.random.fold_in(arg_keys[1], 1), 0, DOC_DEV - 1).astype(jnp.int32),
        "phrase_span": touch_ends(jax.random.randint(arg_keys[2], (PHRASES,), 0, MAX_SPAN + 1), jax.random.fold_in(arg_keys[2], 1), 0, MAX_SPAN).astype(jnp.int32),
        "start_in": scatter_about(arg_keys[3], (H, FFN), H ** -0.5, 0.1875, ((1, 2),)),
        "start_out": scatter_about(arg_keys[4], (FFN, HALF), FFN ** -0.5, 0.1875, ((0, 2),)),
        "end_in": scatter_about(arg_keys[5], (H, FFN), H ** -0.5, 0.1875, ((1, 2),)),
        "end_out": scatter_about(arg_keys[6], (FFN, HALF), FFN ** -0.5, 0.1875, ((0, 2),)),
        "token_table": draw_token_table(jax.random.fold_in(arg_keys[10], 71), 0),
        "queries": draw_queries(jax.random.fold_in(arg_keys[10], 71), 0),
        "targets": touch_ends(jax.random.randint(arg_keys[9], (QUERIES,), 0, PHRASES + V), jax.random.fold_in(arg_keys[9], 1), 0, (PHRASES + V) - 1).astype(jnp.int32),
    }


def phrase_half(rows_in, w_in, w_out):
    hidden = jax.nn.gelu(jnp.dot(rows_in, w_in, preferred_element_type=jnp.float32)).astype(jnp.bfloat16)
    return jnp.dot(hidden, w_out, preferred_element_type=jnp.float32)

def reference(doc_states, phrase_start, phrase_span, start_in, start_out, end_in, end_out, token_table, queries, targets):
    owner = jnp.arange(PHRASES, dtype=jnp.int32) // PH_DP * DOC_DEV
    phrase_end = jnp.minimum(phrase_start + phrase_span, DOC_DEV - 1)
    start_rows = doc_states[owner + phrase_start]
    end_rows = doc_states[owner + phrase_end]
    phrases = jnp.concatenate([phrase_half(start_rows, start_in, start_out), phrase_half(end_rows, end_in, end_out)], axis=1).astype(jnp.bfloat16)
    candidates = jnp.concatenate([phrases, token_table], axis=0)
    factor = 3.0 / math.sqrt(H)
    step_rows = math.gcd(QUERIES, 512)

    def score_block(block_pair):
        query_rows, wanted = block_pair
        scores = jnp.dot(query_rows, candidates.T, preferred_element_type=jnp.float32) * factor
        highest = lax.optimization_barrier(jnp.max(scores, axis=1))
        exp_total = lax.optimization_barrier(jnp.sum(jnp.exp(scores - highest[:, None]), axis=1))
        picked = jnp.take_along_axis(scores, wanted[:, None], axis=1)[:, 0]
        return highest + jnp.log(exp_total) - picked
    losses = lax.map(score_block, (queries.reshape(-1, step_rows, H), targets.reshape(-1, step_rows)))
    return losses.reshape(QUERIES)
```

```python
import functools
import math

import jax
import jax.numpy as jnp
from jax import lax
from jax.experimental import pallas as pl
from jax.experimental.pallas import tpu as pltpu
from jax.sharding import PartitionSpec as P

BF = jnp.bfloat16
F32 = jnp.float32
AXES = ("dp", "mp")
NY, NX = 4, 4
DEVICES = 128
OWN = 128
SLAB = 8
PIECE = OWN + SLAB
WIDTH = 1024
HALF = 512
PHRASES = 65536
CAND = 3072
CHUNK = 512


def coords(n):
    return n // 32, n // 8 % 4, n // 4 % 2, n // 2 % 2, n % 2


def linear(y, x, zh, c, zl):
    return (((y % NY) * NX + x % NX) * 2 + zh) * 4 + c * 2 + zl


def pairs(move):
    return [(n, linear(*move(*coords(n)))) for n in range(DEVICES)]


def send(value, move):
    return lax.ppermute(value, AXES, pairs(move))


def along(first, step):
    def move(y, x, zh, c, zl):
        if (c == 0) == first:
            return y, x + step, zh, c, zl
        return y + step, x, zh, c, zl

    return move


def other_core(y, x, zh, c, zl):
    return y, x, zh, 1 - c, zl


def mp_partner(y, x, zh, c, zl):
    return y, x, zh, c, 1 - zl


def class_partner(y, x, zh, c, zl):
    return y, x, 1 - zh, c, 1 - zl


def owner_groups():
    return [
        [linear(y, x, zh, c, zh ^ k) for y in range(NY) for x in range(NX) for zh in range(2)]
        for c in range(2)
        for k in range(2)
    ]


def phrase_kernel(core_ref, rs_ref, re_ref, si_ref, so_ref, ei_ref, eo_ref, m1_ref, m2_ref, t1_ref, t2_ref,
                  out_ref, si2, ei2, so2, eo2, sems):
    core = core_ref[0]
    copies = []
    for k, (one, two) in enumerate(((m1_ref, m2_ref), (t1_ref, t2_ref))):
        at = core if k == 0 else 1 - core
        big = pl.ds(pl.multiple_of(at * 512, 512), 512)
        small = pl.ds(pl.multiple_of(at * 256, 256), 256)
        copies += [
            pltpu.make_async_copy(one.at[pl.ds(512, 512), :], si2.at[big, :], sems.at[4 * k]),
            pltpu.make_async_copy(two.at[pl.ds(0, 512), :], ei2.at[big, :], sems.at[4 * k + 1]),
            pltpu.make_async_copy(two.at[pl.ds(512, 256), :], so2.at[small, :], sems.at[4 * k + 2]),
            pltpu.make_async_copy(two.at[pl.ds(768, 256), :], eo2.at[small, :], sems.at[4 * k + 3]),
        ]
    for copy in copies:
        copy.start()
    for copy in copies:
        copy.wait()

    def hidden(rows, w):
        return jax.nn.gelu(jnp.dot(rows, w, preferred_element_type=F32)).astype(BF)

    tile = 256

    @pl.loop(0, out_ref.shape[0] // tile)
    def _(r):
        at = pl.ds(pl.multiple_of(r * tile, tile), tile)
        for col, rows_ref, in1, in2, o1, o2 in ((0, rs_ref, si_ref, si2, so_ref, so2), (HALF, re_ref, ei_ref, ei2, eo_ref, eo2)):
            rows = rows_ref[at, :]
            total = jnp.dot(hidden(rows, in1[...]), o1[...], preferred_element_type=F32)
            total += jnp.dot(hidden(rows, in2[...]), o2[...], preferred_element_type=F32)
            out_ref[at, col:col + HALF] = total.astype(BF)


def make_phrases(core, rows_s, rows_e, si, so, ei, eo, mine1, mine2, theirs1, theirs2):
    vm = pl.BlockSpec(memory_space=pltpu.VMEM)
    hbm = pl.BlockSpec(memory_space=pl.ANY)
    n = rows_s.shape[0]
    return pl.pallas_call(
        phrase_kernel,
        in_specs=[pl.BlockSpec(memory_space=pltpu.SMEM)] + [vm] * 6 + [hbm] * 4,
        out_specs=vm,
        out_shape=jax.ShapeDtypeStruct((n, WIDTH), BF),
        scratch_shapes=[
            pltpu.VMEM((WIDTH, 512), BF),
            pltpu.VMEM((WIDTH, 512), BF),
            pltpu.VMEM((512, HALF), BF),
            pltpu.VMEM((512, HALF), BF),
            pltpu.SemaphoreType.DMA((8,)),
        ],
        compiler_params=pltpu.CompilerParams(vmem_limit_bytes=40 << 20),
        cost_estimate=pl.CostEstimate(flops=6_500_000_000, bytes_accessed=12 << 20, transcendentals=2 << 20),
        name="phrases",
    )(core, rows_s, rows_e, si, so, ei, eo, mine1, mine2, theirs1, theirs2)


def score_kernel(factor, base_ref, qa_ref, qb_ref, tok_ref, tokc_ref, tz_ref, tzc_ref, ph_ref, phc_ref,
                 out_ref, cand, qbuf, csem, qsem):
    qcopies = [
        pltpu.make_async_copy(qa_ref, qbuf.at[0], qsem.at[0]),
        pltpu.make_async_copy(qb_ref, qbuf.at[1], qsem.at[1]),
    ]
    r256 = pl.ds(0, 256)
    plan = [
        (0, tok_ref, cand.at[pl.ds(0, 256), :]),
        (0, tokc_ref, cand.at[pl.ds(256, 256), :]),
        (1, tz_ref.at[r256, :], cand.at[pl.ds(512, 256), pl.ds(0, 512)]),
        (1, tz_ref.at[pl.ds(256, 256), :], cand.at[pl.ds(512, 256), pl.ds(512, 512)]),
        (1, tzc_ref.at[r256, :], cand.at[pl.ds(768, 256), pl.ds(0, 512)]),
        (1, tzc_ref.at[pl.ds(256, 256), :], cand.at[pl.ds(768, 256), pl.ds(512, 512)]),
    ]
    for j in range(2):
        plan.append((2 + j, ph_ref.at[pl.ds(j * 512, 512), :], cand.at[pl.ds(1024 + j * 512, 512), :]))
    for j in range(2):
        plan.append((4 + j, phc_ref.at[pl.ds(j * 512, 512), :], cand.at[pl.ds(2048 + j * 512, 512), :]))
    ccopies = [(chunk, pltpu.make_async_copy(src, dst, csem.at[i])) for i, (chunk, src, dst) in enumerate(plan)]
    qcopies[0].start()
    for _, copy in ccopies:
        copy.start()
    qcopies[1].start()

    rows = 4 * OWN
    lane = lax.broadcasted_iota(jnp.int32, (1, 128), 1)
    eye = lax.broadcasted_iota(jnp.int32, (OWN, OWN), 0) == lax.broadcasted_iota(jnp.int32, (OWN, OWN), 1)
    k2 = factor * math.log2(math.e)
    for tile in range(2):
        qcopies[tile].wait()
        q = qbuf[tile, :, 0:OWN, :].reshape(rows, WIDTH)
        wanted = []
        for p in range(4):
            digits = qbuf[tile, p, OWN:PIECE, 0:384].astype(F32)[0:1, :]
            row = (digits[:, 0:128] * 65536.0 + digits[:, 128:256] * 256.0 + digits[:, 256:384])
            col = jnp.sum(jnp.where(eye, jnp.broadcast_to(row, (OWN, OWN)), 0.0), axis=1, keepdims=True)
            wanted.append(jnp.broadcast_to(col.astype(jnp.int32), (OWN, 128)))
        wanted = jnp.concatenate(wanted, axis=0)
        high = jnp.full((rows, 128), -jnp.inf, F32)
        total = jnp.zeros((rows, 128), F32)
        picked = jnp.zeros((rows, 128), F32)
        for j in range(CAND // CHUNK):
            if tile == 0:
                for chunk, copy in ccopies:
                    if chunk == j:
                        copy.wait()
            sc = lax.dot_general(
                q, cand[j * CHUNK:(j + 1) * CHUNK, :], (((1,), (1,)), ((), ())), preferred_element_type=F32
            )
            groups = [sc[:, i * 128:(i + 1) * 128] for i in range(CHUNK // 128)]
            new_high = jnp.maximum(high, functools.reduce(jnp.maximum, groups))
            fresh = functools.reduce(jnp.add, [jnp.exp2((g - new_high) * k2) for g in groups])
            total = fresh if j == 0 else total * jnp.exp2((high - new_high) * k2) + fresh
            high = new_high
            for i, g in enumerate(groups):
                at = j * CHUNK + i * 128
                picked = jnp.where(wanted == lane + (base_ref[at // 256] + at % 256), g, picked)
        top = jnp.max(high, axis=1, keepdims=True)
        summed = jnp.sum(total * jnp.exp2((high - top) * k2), axis=1, keepdims=True)
        lse = top * factor + jnp.log(summed)
        score = jnp.sum(picked, axis=1, keepdims=True) * factor
        for p in range(4):
            at = slice(p * OWN, (p + 1) * OWN)
            out_ref[tile * 4 + p, 0:1, :] = lse[at].reshape(1, OWN)
            out_ref[tile * 4 + p, 1:2, :] = score[at].reshape(1, OWN)


def block_stats(factor, bases, qa, qb, cands):
    hbm = pl.BlockSpec(memory_space=pl.ANY)
    rows = 8 * OWN
    return pl.pallas_call(
        functools.partial(score_kernel, factor),
        in_specs=[pl.BlockSpec(memory_space=pltpu.SMEM)] + [hbm] * 8,
        out_specs=pl.BlockSpec(memory_space=pltpu.VMEM),
        out_shape=jax.ShapeDtypeStruct((8, 2, OWN), F32),
        scratch_shapes=[
            pltpu.VMEM((CAND, WIDTH), BF),
            pltpu.VMEM((2, 4, PIECE, WIDTH), BF),
            pltpu.SemaphoreType.DMA((10,)),
            pltpu.SemaphoreType.DMA((2,)),
        ],
        compiler_params=pltpu.CompilerParams(vmem_limit_bytes=48 << 20),
        cost_estimate=pl.CostEstimate(
            flops=2 * rows * CAND * WIDTH, bytes_accessed=9 << 20, transcendentals=rows * CAND
        ),
        name="scores",
    )(bases, qa, qb, *cands)


def per_device(doc_states, phrase_start, phrase_span, start_in, start_out, end_in, end_out, token_table, queries, targets):
    factor = 3.0 / math.sqrt(WIDTH)
    dp = lax.axis_index("dp")
    mp = lax.axis_index("mp")
    core = dp % 2

    digits = jnp.concatenate([targets // 65536, targets // 256 % 256, targets % 256]).astype(BF)
    slab = jnp.zeros((SLAB, WIDTH), BF).at[0, 0:3 * OWN].set(digits)
    own = jnp.concatenate([queries, slab], axis=0)[None]
    from_z = send(own, class_partner)

    tok2 = jnp.concatenate([token_table[:, :512], token_table[:, 512:]], axis=0)
    big = lambda w: lax.dynamic_slice_in_dim(w, core * 512, 512, axis=0)
    small = lambda w: lax.dynamic_slice_in_dim(w, core * 256, 256, axis=0)
    mine1 = send(jnp.concatenate([tok2, big(start_in)], axis=0), mp_partner)
    mine2 = send(jnp.concatenate([big(end_in), small(start_out), small(end_out)], axis=0), class_partner)
    tokens_c = send(token_table, other_core)

    base = jnp.concatenate([own, from_z], axis=0)
    left = send(base, along(True, 1))
    right = send(base, along(True, -1))
    far = send(base, along(True, 2))
    part1 = jnp.concatenate([base, left], axis=0)
    part2 = jnp.concatenate([right, far], axis=0)
    u1 = send(part1, along(False, 1))
    d1 = send(part1, along(False, -1))
    u2 = send(part2, along(False, 1))
    d2 = send(part2, along(False, -1))
    f1 = send(u1, along(False, 1))
    f2 = send(d2, along(False, -1))

    phrase_end = jnp.minimum(phrase_start + phrase_span, doc_states.shape[0] - 1)
    start_rows = jnp.take(doc_states, phrase_start, axis=0, mode="clip")
    end_rows = jnp.take(doc_states, phrase_end, axis=0, mode="clip")
    theirs1 = send(mine1, other_core)
    theirs2 = send(mine2, other_core)
    phrases = make_phrases(
        core.reshape(1), start_rows, end_rows, start_in, start_out, end_in, end_out, mine1, mine2, theirs1, theirs2
    )
    phrases_c = send(phrases, other_core)

    device = dp * 2 + mp
    quarter = jnp.arange(4, dtype=jnp.int32) * 256
    bases = jnp.concatenate([
        PHRASES + (device ^ jnp.array([0, 2, 1, 3], jnp.int32)) * 256,
        dp * 1024 + quarter,
        (dp ^ 1) * 1024 + quarter,
    ]).astype(jnp.int32)
    cands = (token_table, tokens_c, mine1, theirs1, phrases, phrases_c)
    stats = [
        block_stats(factor, bases, part1, part2, cands),
        block_stats(factor, bases, u1, d1, cands),
        block_stats(factor, bases, u2, d2, cands),
        block_stats(factor, bases, f1, f2, cands),
    ]
    stats = jnp.concatenate(stats, axis=0)

    y, x, zh = dp // 16, dp // 4 % 4, dp // 2 % 2
    n = jnp.arange(32, dtype=jnp.int32)
    dy, dx, s = (n // 8 - y) % 4, (n // 2 - x) % 4, (n % 2) ^ zh
    i = jnp.where(core == 0, dx, dy)
    j = jnp.where(core == 0, dy, dx)
    first = jnp.where(i == 3, 1, jnp.where(i == 1, 2, jnp.where(i == 2, 3, 0)))
    second = first // 2
    array = jnp.where(j == 0, second, jnp.where(j == 3, 2 + 2 * second, jnp.where(j == 1, 3 + 2 * second, 6 + second)))
    place = array * 4 + (first % 2) * 2 + s
    ordered = jnp.take(stats, place, axis=0, mode="clip")
    received = lax.all_to_all(
        ordered, AXES, split_axis=0, concat_axis=0, tiled=True, axis_index_groups=owner_groups()
    )
    lse, score = received[:, 0, :], received[:, 1, :]
    top = jnp.max(lse, axis=0)
    return top + jnp.log(jnp.sum(jnp.exp(lse - top[None, :]), axis=0)) - jnp.sum(score, axis=0)


def solution(mesh):
    in_specs = (
        P("dp", None),
        P("dp"),
        P("dp"),
        P(None, "mp"),
        P("mp", None),
        P(None, "mp"),
        P("mp", None),
        P(("dp", "mp"), None),
        P(("dp", "mp"), None),
        P(("dp", "mp")),
    )
    return jax.shard_map(
        per_device, mesh=mesh, in_specs=in_specs, out_specs=P(("dp", "mp")), check_vma=False
    )
```

```python
import functools
import math

import jax
import jax.numpy as jnp
from jax import lax
from jax.experimental import pallas as pl
from jax.experimental.pallas import tpu as pltpu
from jax.sharding import PartitionSpec as P

BF = jnp.bfloat16
F32 = jnp.float32
AXES = ("dp", "mp")
NY, NX = 4, 4
DEVICES = 128
OWN = 128
SLAB = 8
PIECE = OWN + SLAB
WIDTH = 1024
HALF = 512
PHRASES = 65536
CHUNK = 512


def coords(n):
    return n // 32, n // 8 % 4, n // 4 % 2, n // 2 % 2, n % 2


def linear(y, x, zh, c, zl):
    return (((y % NY) * NX + x % NX) * 2 + zh) * 4 + c * 2 + zl


def pairs(move):
    return [(n, linear(*move(*coords(n)))) for n in range(DEVICES)]


def send(value, move):
    return lax.ppermute(value, AXES, pairs(move))


def along(first, step):
    def move(y, x, zh, c, zl):
        if (c == 0) == first:
            return y, x + step, zh, c, zl
        return y + step, x, zh, c, zl

    return move


def other_core(y, x, zh, c, zl):
    return y, x, zh, 1 - c, zl


def mp_partner(y, x, zh, c, zl):
    return y, x, zh, c, 1 - zl


def class_partner(y, x, zh, c, zl):
    return y, x, 1 - zh, c, 1 - zl


def owner_groups():
    return [
        [linear(y, x, zh, c, zh ^ k) for y in range(NY) for x in range(NX) for zh in range(2)]
        for c in range(2)
        for k in range(2)
    ]


def vm_copy(src, dst, sems, k):
    return pltpu.make_async_copy(src, dst, sems.at[k])


ANY = pl.BlockSpec(memory_space=pl.ANY)
SMEM = pl.BlockSpec(memory_space=pltpu.SMEM)
VMEM = pl.BlockSpec(memory_space=pltpu.VMEM)
SMALL = pl.CostEstimate(flops=1 << 20, bytes_accessed=1 << 16, transcendentals=0)


def in_hbm(*arrays):
    return [pltpu.with_memory_space_constraint(array, pltpu.HBM) for array in arrays]


ROWS_ONE, ROWS_TWO = 1152, 896


def pack_kernel(core_ref, tok_ref, si_ref, so_ref, ei_ref, eo_ref, one_ref, two_ref, one, two, sems):
    at = pl.multiple_of(core_ref[0] * 512, 512)
    small = pl.ds(pl.multiple_of(core_ref[0] * 256, 256), 256)
    loads = [
        vm_copy(src, dst, sems, k)
        for k, (src, dst) in enumerate((
            (si_ref.at[pl.ds(at + 128, 384), :], two.at[pl.ds(0, 384), :]),
            (ei_ref.at[pl.ds(at, 512), :], two.at[pl.ds(384, 512), :]),
            (tok_ref.at[:, pl.ds(0, 512)], one.at[pl.ds(0, 256), :]),
            (tok_ref.at[:, pl.ds(512, 512)], one.at[pl.ds(256, 256), :]),
            (so_ref.at[small, :], one.at[pl.ds(512, 256), :]),
            (eo_ref.at[small, :], one.at[pl.ds(768, 256), :]),
            (si_ref.at[pl.ds(at, 128), :], one.at[pl.ds(1024, 128), :]),
        ))
    ]
    stores = [vm_copy(two, two_ref, sems, 7), vm_copy(one, one_ref, sems, 8)]
    for load in loads:
        load.start()
    for load in loads[:2]:
        load.wait()
    stores[0].start()
    for load in loads[2:]:
        load.wait()
    stores[1].start()
    for store in stores:
        store.wait()


def pack(core, tokens, si, so, ei, eo):
    return pl.pallas_call(
        pack_kernel,
        in_specs=[SMEM] + [ANY] * 5,
        out_specs=[ANY] * 2,
        out_shape=[jax.ShapeDtypeStruct((n, 512), BF) for n in (ROWS_ONE, ROWS_TWO)],
        scratch_shapes=[pltpu.VMEM((n, 512), BF) for n in (ROWS_ONE, ROWS_TWO)] + [pltpu.SemaphoreType.DMA((9,))],
        compiler_params=pltpu.CompilerParams(vmem_limit_bytes=8 << 20),
        cost_estimate=SMALL,
        name="pack",
    )(core, *in_hbm(tokens, si, so, ei, eo))


def join_kernel(spans, *refs):
    ins, out, held, sems = refs[:len(spans)], refs[-3], refs[-2], refs[-1]
    loads, stores, at = [], [], 0
    for k, (first, n) in enumerate(spans):
        here = pl.ds(at, n)
        loads.append(vm_copy(ins[k].at[pl.ds(first, n)], held.at[here], sems, (0, k)))
        stores.append(vm_copy(held.at[here], out.at[here], sems, (1, k)))
        at += n
    for load in loads:
        load.start()
    for load, store in zip(loads, stores):
        load.wait()
        store.start()
    for store in stores:
        store.wait()


def join(parts, spans=None):
    spans = spans or [(0, part.shape[0]) for part in parts]
    shape = (sum(n for _, n in spans),) + parts[0].shape[1:]
    return pl.pallas_call(
        functools.partial(join_kernel, tuple(spans)),
        in_specs=[ANY] * len(parts),
        out_specs=ANY,
        out_shape=jax.ShapeDtypeStruct(shape, parts[0].dtype),
        scratch_shapes=[pltpu.VMEM(shape, parts[0].dtype), pltpu.SemaphoreType.DMA((2, len(parts)))],
        compiler_params=pltpu.CompilerParams(vmem_limit_bytes=8 << 20),
        cost_estimate=SMALL,
        name="join",
    )(*in_hbm(*parts))


def phrase_kernel(extra, core_ref, rows_ref, si_ref, so_ref, ei_ref, eo_ref, m1_ref, m2_ref, t1_ref, t2_ref, *refs):
    out_hbm, out_ref, rows, si, so, ei, eo, si2, so2, ei2, eo2, sems = refs[extra:]
    n = out_hbm.shape[0]
    core = core_ref[0]
    parts = [(rows_ref.at[pl.ds(0, n), :], rows.at[pl.ds(0, n), :]), (si_ref, si), (so_ref, so),
             (rows_ref.at[pl.ds(n, n), :], rows.at[pl.ds(n, n), :]), (ei_ref, ei), (eo_ref, eo)]
    from_start, from_end = [], []
    for c, one, two in ((core, m1_ref, m2_ref), (1 - core, t1_ref, t2_ref)):
        at = pl.multiple_of(c * 512, 512)
        small = pl.ds(pl.multiple_of(c * 256, 256), 256)
        from_start += [
            (one.at[pl.ds(512, 256), :], so2.at[small, :]),
            (one.at[pl.ds(1024, 128), :], si2.at[pl.ds(at, 128), :]),
            (two.at[pl.ds(0, 384), :], si2.at[pl.ds(at + 128, 384), :]),
        ]
        from_end += [
            (one.at[pl.ds(768, 256), :], eo2.at[small, :]),
            (two.at[pl.ds(384, 512), :], ei2.at[pl.ds(at, 512), :]),
        ]
    parts = parts[:3] + from_start + parts[3:] + from_end
    copies = [vm_copy(src, dst, sems, k) for k, (src, dst) in enumerate(parts)]
    for copy in copies:
        copy.start()

    def hidden(at, w):
        return jax.nn.gelu(jnp.dot(rows[at, :], w[...], preferred_element_type=F32)).astype(BF)

    tile = n // 2
    for half, (in1, out1, in2, out2) in enumerate(((si, so, si2, so2), (ei, eo, ei2, eo2))):
        for k in range(9 * half, 9 * half + 3):
            copies[k].wait()
        for r in range(2):
            at = slice(half * n + r * tile, half * n + (r + 1) * tile)
            total = jnp.dot(hidden(at, in1), out1[...], preferred_element_type=F32)
            if r == 0:
                for k in ((3, 4, 5, 6, 7, 8), (12, 13, 14, 15))[half]:
                    copies[k].wait()
            total += jnp.dot(hidden(at, in2), out2[...], preferred_element_type=F32)
            out_ref[r * tile:(r + 1) * tile, half * HALF:(half + 1) * HALF] = total.astype(BF)
    done = vm_copy(out_ref, out_hbm, sems, 16)
    done.start()
    done.wait()


def make_phrases(core, rows, si, so, ei, eo, mine1, mine2, theirs1, theirs2, after=()):
    n = rows.shape[0] // 2
    weights = [pltpu.VMEM((WIDTH, 512), BF), pltpu.VMEM((512, HALF), BF)] * 4
    return pl.pallas_call(
        functools.partial(phrase_kernel, len(after)),
        in_specs=[SMEM] + [ANY] * (9 + len(after)),
        out_specs=ANY,
        out_shape=jax.ShapeDtypeStruct((n, WIDTH), BF),
        scratch_shapes=[pltpu.VMEM((n, WIDTH), BF), pltpu.VMEM((2 * n, WIDTH), BF)] + weights
        + [pltpu.SemaphoreType.DMA((17,))],
        compiler_params=pltpu.CompilerParams(vmem_limit_bytes=22 << 20),
        cost_estimate=SMALL,
        name="phrases",
    )(core, *in_hbm(rows, si, so, ei, eo, mine1, mine2, theirs1, theirs2), *after)


def score_kernel(factor, count, base_ref, *refs):
    q_refs, (tok_ref, tokc_ref, m1_ref, t1_ref, own_ref, oth_ref, out_ref, ztok) = refs[:-8], refs[-8:]
    lane = lax.broadcasted_iota(jnp.int32, (1, 128), 1)
    eye = lax.broadcasted_iota(jnp.int32, (OWN, OWN), 0) == lax.broadcasted_iota(jnp.int32, (OWN, OWN), 1)
    k2 = factor * math.log2(math.e)
    for k, ref in enumerate((m1_ref, t1_ref)):
        for h in range(2):
            ztok[k * 256:(k + 1) * 256, h * 512:(h + 1) * 512] = ref[h * 256:(h + 1) * 256, :]
    blocks = [(own_ref, 0, 4), (own_ref, 512, 6), (oth_ref, 0, 8), (oth_ref, 512, 10)]
    spread = [(q_ref, at) for q_ref in q_refs for at in range(0, q_ref.shape[0], count)]
    for tile, (q_ref, first) in enumerate(spread):
        pieces = range(first, first + count)
        rows = count * OWN
        q = q_ref[first:first + count, 0:OWN, :].reshape(rows, WIDTH)
        wanted = []
        for p in pieces:
            found = q_ref[p, OWN:PIECE, 0:384].astype(F32)[0:1, :]
            row = (found[:, 0:128] * 65536.0 + found[:, 128:256] * 256.0 + found[:, 256:384])
            col = jnp.sum(jnp.where(eye, jnp.broadcast_to(row, (OWN, OWN)), 0.0), axis=1, keepdims=True)
            wanted.append(jnp.broadcast_to(col.astype(jnp.int32), (OWN, 128)))
        wanted = jnp.concatenate(wanted, axis=0)
        high = jnp.full((rows, 128), -jnp.inf, F32)
        total = jnp.zeros((rows, 128), F32)
        picked = jnp.zeros((rows, 128), F32)
        for j in range(6):
            if j == 0:
                c = jnp.concatenate([tok_ref[...], tokc_ref[...]], axis=0)
            elif j == 1:
                c = ztok[...]
            else:
                ref, at, _ = blocks[j - 2]
                c = ref[at:at + CHUNK, :]
            sc = lax.dot_general(q, c, (((1,), (1,)), ((), ())), preferred_element_type=F32)
            groups = [sc[:, i * 128:(i + 1) * 128] for i in range(CHUNK // 128)]
            new_high = jnp.maximum(high, functools.reduce(jnp.maximum, groups))
            fresh = functools.reduce(jnp.add, [jnp.exp2((g - new_high) * k2) for g in groups])
            total = fresh if j == 0 else total * jnp.exp2((high - new_high) * k2) + fresh
            high = new_high
            for i, g in enumerate(groups):
                picked = jnp.where(wanted == lane + (base_ref[2 * j + i // 2] + i % 2 * 128), g, picked)
        top = jnp.max(high, axis=1, keepdims=True)
        summed = jnp.sum(total * jnp.exp2((high - top) * k2), axis=1, keepdims=True)
        lse = top * factor + jnp.log(summed)
        score = jnp.sum(picked, axis=1, keepdims=True) * factor
        for p in range(count):
            at = slice(p * OWN, (p + 1) * OWN)
            out_ref[tile * count + p, 0:1, :] = lse[at].reshape(1, OWN)
            out_ref[tile * count + p, 1:2, :] = score[at].reshape(1, OWN)


def block_stats(factor, bases, queries, candidates, count=8):
    pieces = sum(q.shape[0] for q in queries)
    return pl.pallas_call(
        functools.partial(score_kernel, factor, count),
        in_specs=[SMEM] + [VMEM] * (len(queries) + len(candidates)),
        out_specs=VMEM,
        out_shape=jax.ShapeDtypeStruct((pieces, 2, OWN), F32),
        scratch_shapes=[pltpu.VMEM((512, WIDTH), BF)],
        compiler_params=pltpu.CompilerParams(vmem_limit_bytes=20 << 20),
        cost_estimate=SMALL,
        name="scores",
    )(bases, *queries, *candidates)


def after(value, *earlier):
    return lax.optimization_barrier((value,) + earlier)[0]


def per_device(doc_states, phrase_start, phrase_span, start_in, start_out, end_in, end_out, token_table, queries, targets):
    factor = 3.0 / math.sqrt(WIDTH)
    dp = lax.axis_index("dp")
    mp = lax.axis_index("mp")
    core = dp % 2
    device = dp * 2 + mp

    digits = jnp.concatenate([targets // 65536, targets // 256 % 256, targets % 256]).astype(BF)
    slab = jnp.zeros((SLAB, WIDTH), BF).at[0, 0:3 * OWN].set(digits)
    own = jnp.concatenate([queries, slab], axis=0)[None]
    from_z = send(own, class_partner)

    core_ref = core.reshape(1)
    pay1, pay2 = pack(after(core_ref, own), token_table, start_in, start_out, end_in, end_out)
    mine2 = send(pay2, class_partner)
    mine1 = send(pay1, mp_partner)
    tokens_c = send(token_table, other_core)

    base = jnp.concatenate([own, after(from_z, pay1)], axis=0)
    left = send(base, along(True, 1))
    right = send(base, along(True, -1))
    far = send(base, along(True, 2))

    ends = jnp.minimum(phrase_start + phrase_span, doc_states.shape[0] - 1)
    index = jnp.concatenate([phrase_start, ends])
    rows = jnp.take(doc_states, after(index, base), axis=0, mode="clip")

    part = join([base, after(left, rows), right, far])
    up = send(part, along(False, 1))
    down = send(part, along(False, -1))

    mine1, mine2 = after(mine1, part), after(mine2, part)
    theirs1 = send(mine1, other_core)
    theirs2 = send(mine2, other_core)
    phrases = make_phrases(
        core_ref, rows, start_in, start_out, end_in, end_out, mine1, mine2, theirs1, theirs2
    )
    phrases_c = send(phrases, other_core)

    quarters = jnp.arange(4, dtype=jnp.int32) * 256
    bases = jnp.concatenate([
        PHRASES + (device ^ jnp.array([0, 2, 1, 3], jnp.int32)) * 256, dp * 1024 + quarters, (dp ^ 1) * 1024 + quarters
    ]).astype(jnp.int32)
    candidates = (token_table, tokens_c, mine1, theirs1, phrases, phrases_c)
    stats1 = block_stats(factor, bases, [part], candidates)
    up, down = after(up, stats1), after(down, stats1)
    far1 = send(join([up], [(0, 4)]), along(False, 1))
    far2 = send(join([down], [(4, 4)]), along(False, -1))
    stats2 = block_stats(factor, bases, [up, down], candidates)
    stats3 = block_stats(factor, bases, [after(far1, stats2), far2], candidates, count=4)
    stats = jnp.concatenate([stats1, stats2, stats3], axis=0)

    y, x, zh = dp // 16, dp // 4 % 4, dp // 2 % 2
    n = jnp.arange(32, dtype=jnp.int32)
    dy, dx, s = (n // 8 - y) % 4, (n // 2 - x) % 4, (n % 2) ^ zh
    i = jnp.where(core == 0, dx, dy)
    j = jnp.where(core == 0, dy, dx)
    first = jnp.where(i == 3, 1, jnp.where(i == 1, 2, jnp.where(i == 2, 3, 0)))
    block = jnp.where(j == 0, 0, jnp.where(j == 3, 1, jnp.where(j == 1, 2, 3)))
    place = block * 8 + first * 2 + s
    ordered = jnp.take(stats, place, axis=0, mode="clip")
    received = lax.all_to_all(
        ordered, AXES, split_axis=0, concat_axis=0, tiled=True, axis_index_groups=owner_groups()
    )
    lse, score = received[:, 0, :], received[:, 1, :]
    top = jnp.max(lse, axis=0)
    return top + jnp.log(jnp.sum(jnp.exp(lse - top[None, :]), axis=0)) - jnp.sum(score, axis=0)


def solution(mesh):
    in_specs = (
        P("dp", None),
        P("dp"),
        P("dp"),
        P(None, "mp"),
        P("mp", None),
        P(None, "mp"),
        P("mp", None),
        P(("dp", "mp"), None),
        P(("dp", "mp"), None),
        P(("dp", "mp")),
    )
    return jax.shard_map(
        per_device, mesh=mesh, in_specs=in_specs, out_specs=P(("dp", "mp")), check_vma=False
    )
```

```python
import functools
import math

import jax
import jax.numpy as jnp
from jax import lax
from jax.experimental import pallas as pl
from jax.experimental.pallas import tpu as pltpu
from jax.sharding import PartitionSpec as P

BF = jnp.bfloat16
F32 = jnp.float32
AXES = ("dp", "mp")
NY, NX = 4, 4
DEVICES = 128
OWN = 128
SLAB = 8
PIECE = OWN + SLAB
WIDTH = 1024
HALF = 512
PHRASES = 65536
CHUNK = 512


def coords(n):
    return n // 32, n // 8 % 4, n // 4 % 2, n // 2 % 2, n % 2


def linear(y, x, zh, c, zl):
    return (((y % NY) * NX + x % NX) * 2 + zh) * 4 + c * 2 + zl


def pairs(move):
    return [(n, linear(*move(*coords(n)))) for n in range(DEVICES)]


def send(value, move):
    return lax.ppermute(value, AXES, pairs(move))


def along(first, step):
    def move(y, x, zh, c, zl):
        if (c == 0) == first:
            return y, x + step, zh, c, zl
        return y + step, x, zh, c, zl

    return move


def other_core(y, x, zh, c, zl):
    return y, x, zh, 1 - c, zl


def mp_partner(y, x, zh, c, zl):
    return y, x, zh, c, 1 - zl


def class_partner(y, x, zh, c, zl):
    return y, x, 1 - zh, c, 1 - zl


def owner_groups():
    return [
        [linear(y, x, zh, c, zh ^ k) for y in range(NY) for x in range(NX) for zh in range(2)]
        for c in range(2)
        for k in range(2)
    ]


def vm_copy(src, dst, sems, k):
    return pltpu.make_async_copy(src, dst, sems.at[k])


ANY = pl.BlockSpec(memory_space=pl.ANY)
SMEM = pl.BlockSpec(memory_space=pltpu.SMEM)
VMEM = pl.BlockSpec(memory_space=pltpu.VMEM)
SMALL = pl.CostEstimate(flops=1 << 20, bytes_accessed=1 << 16, transcendentals=0)


def in_hbm(*arrays):
    return [pltpu.with_memory_space_constraint(array, pltpu.HBM) for array in arrays]


ROWS_ONE, ROWS_TWO = 1152, 896


def pack_kernel(core_ref, tgt_ref, q_ref, tok_ref, si_ref, so_ref, ei_ref, eo_ref, own_ref, one_ref, two_ref, one, two, sems):
    queries = vm_copy(q_ref, own_ref.at[0, pl.ds(0, OWN), :], sems, 9)
    queries.start()
    at = pl.multiple_of(core_ref[0] * 512, 512)
    small = pl.ds(pl.multiple_of(core_ref[0] * 256, 256), 256)
    loads = [
        vm_copy(src, dst, sems, k)
        for k, (src, dst) in enumerate((
            (si_ref.at[pl.ds(at + 128, 384), :], two.at[pl.ds(0, 384), :]),
            (ei_ref.at[pl.ds(at, 512), :], two.at[pl.ds(384, 512), :]),
            (tok_ref.at[:, pl.ds(0, 512)], one.at[pl.ds(0, 256), :]),
            (tok_ref.at[:, pl.ds(512, 512)], one.at[pl.ds(256, 256), :]),
            (so_ref.at[small, :], one.at[pl.ds(512, 256), :]),
            (eo_ref.at[small, :], one.at[pl.ds(768, 256), :]),
            (si_ref.at[pl.ds(at, 128), :], one.at[pl.ds(1024, 128), :]),
        ))
    ]
    for load in loads:
        load.start()
    target = tgt_ref[...]
    digits = [jnp.right_shift(target, 16), jnp.bitwise_and(jnp.right_shift(target, 8), 255), jnp.bitwise_and(target, 255)]
    row = jnp.concatenate(digits + [jnp.zeros((1, WIDTH - 3 * OWN), jnp.int32)], axis=1).astype(F32)
    own_ref[0, OWN:PIECE, :] = jnp.broadcast_to(row, (SLAB, WIDTH)).astype(BF)
    stores = [vm_copy(two, two_ref, sems, 7), vm_copy(one, one_ref, sems, 8)]
    for load in loads[:2]:
        load.wait()
    stores[0].start()
    for load in loads[2:]:
        load.wait()
    stores[1].start()
    for store in stores:
        store.wait()
    queries.wait()


def pack(core, targets, queries, tokens, si, so, ei, eo):
    return pl.pallas_call(
        pack_kernel,
        in_specs=[SMEM, VMEM] + [ANY] * 6,
        out_specs=[VMEM, ANY, ANY],
        out_shape=[jax.ShapeDtypeStruct((1, PIECE, WIDTH), BF)]
        + [jax.ShapeDtypeStruct((n, 512), BF) for n in (ROWS_ONE, ROWS_TWO)],
        scratch_shapes=[pltpu.VMEM((n, 512), BF) for n in (ROWS_ONE, ROWS_TWO)] + [pltpu.SemaphoreType.DMA((10,))],
        compiler_params=pltpu.CompilerParams(vmem_limit_bytes=8 << 20),
        cost_estimate=SMALL,
        name="pack",
    )(core, targets.reshape(1, OWN), *in_hbm(queries, tokens, si, so, ei, eo))


def join_kernel(spans, *refs):
    ins, out, sems = refs[:len(spans)], refs[-2], refs[-1]
    loads, at = [], 0
    for k, (first, n) in enumerate(spans):
        loads.append(vm_copy(ins[k].at[pl.ds(first, n)], out.at[pl.ds(at, n)], sems, k))
        at += n
    for load in loads:
        load.start()
    for load in loads:
        load.wait()


def join(parts, spans=None):
    spans = spans or [(0, part.shape[0]) for part in parts]
    shape = (sum(n for _, n in spans),) + parts[0].shape[1:]
    return pl.pallas_call(
        functools.partial(join_kernel, tuple(spans)),
        in_specs=[ANY] * len(parts),
        out_specs=VMEM,
        out_shape=jax.ShapeDtypeStruct(shape, parts[0].dtype),
        scratch_shapes=[pltpu.SemaphoreType.DMA((len(parts),))],
        compiler_params=pltpu.CompilerParams(vmem_limit_bytes=8 << 20),
        cost_estimate=SMALL,
        name="join",
    )(*in_hbm(*parts))


def phrase_kernel(core_ref, rows_ref, si_ref, so_ref, ei_ref, eo_ref, m1_ref, m2_ref, t1_ref, t2_ref, tok_ref, tokc_ref,
                  out_ref, tokens_ref, rows, si, so, ei, eo, si2, so2, ei2, eo2, tokens, sems):
    n = rows_ref.shape[0] // 2
    core = core_ref[0]
    parts = [(rows_ref.at[pl.ds(0, n), :], rows.at[pl.ds(0, n), :]), (si_ref, si), (so_ref, so),
             (rows_ref.at[pl.ds(n, n), :], rows.at[pl.ds(n, n), :]), (ei_ref, ei), (eo_ref, eo)]
    from_start, from_end = [], []
    for c, one, two in ((core, m1_ref, m2_ref), (1 - core, t1_ref, t2_ref)):
        at = pl.multiple_of(c * 512, 512)
        small = pl.ds(pl.multiple_of(c * 256, 256), 256)
        from_start += [
            (one.at[pl.ds(512, 256), :], so2.at[small, :]),
            (one.at[pl.ds(1024, 128), :], si2.at[pl.ds(at, 128), :]),
            (two.at[pl.ds(0, 384), :], si2.at[pl.ds(at + 128, 384), :]),
        ]
        from_end += [
            (one.at[pl.ds(768, 256), :], eo2.at[small, :]),
            (two.at[pl.ds(384, 512), :], ei2.at[pl.ds(at, 512), :]),
        ]
    parts = parts[:3] + from_start + parts[3:] + from_end
    parts += [(tok_ref, tokens.at[pl.ds(0, 256), :]), (tokc_ref, tokens.at[pl.ds(256, 256), :])]
    parts += [
        (one.at[pl.ds(h * 256, 256), :], tokens.at[pl.ds(512 + 256 * k, 256), pl.ds(h * 512, 512)])
        for k, one in enumerate((m1_ref, t1_ref)) for h in range(2)
    ]
    copies = [vm_copy(src, dst, sems, k) for k, (src, dst) in enumerate(parts)]
    for copy in copies:
        copy.start()

    def hidden(at, w):
        return jax.nn.gelu(jnp.dot(rows[at, :], w[...], preferred_element_type=F32)).astype(BF)

    tile = n // 2
    for half, (in1, out1, in2, out2) in enumerate(((si, so, si2, so2), (ei, eo, ei2, eo2))):
        for k in range(9 * half, 9 * half + 3):
            copies[k].wait()
        if half:
            for copy in copies[16:]:
                copy.wait()
            stored = vm_copy(tokens, tokens_ref, sems, 22)
            stored.start()
        for r in range(2):
            at = slice(half * n + r * tile, half * n + (r + 1) * tile)
            total = jnp.dot(hidden(at, in1), out1[...], preferred_element_type=F32)
            if r == 0:
                for k in ((3, 4, 5, 6, 7, 8), (12, 13, 14, 15))[half]:
                    copies[k].wait()
            total += jnp.dot(hidden(at, in2), out2[...], preferred_element_type=F32)
            out_ref[r * tile:(r + 1) * tile, half * HALF:(half + 1) * HALF] = total.astype(BF)
    stored.wait()


def make_phrases(core, rows, si, so, ei, eo, mine1, mine2, theirs1, theirs2, token_table, tokens_c):
    n = rows.shape[0] // 2
    weights = [pltpu.VMEM((WIDTH, 512), BF), pltpu.VMEM((512, HALF), BF)] * 4
    tokens = (4 * token_table.shape[0], WIDTH)
    return pl.pallas_call(
        phrase_kernel,
        in_specs=[SMEM] + [ANY] * 11,
        out_specs=[VMEM, ANY],
        out_shape=[jax.ShapeDtypeStruct((n, WIDTH), BF), pltpu.HBM(tokens, BF)],
        scratch_shapes=[pltpu.VMEM((2 * n, WIDTH), BF)] + weights
        + [pltpu.VMEM(tokens, BF), pltpu.SemaphoreType.DMA((23,))],
        compiler_params=pltpu.CompilerParams(vmem_limit_bytes=24 << 20),
        cost_estimate=SMALL,
        name="phrases",
    )(core, *in_hbm(rows, si, so, ei, eo), mine1, *in_hbm(mine2), theirs1, theirs2, *in_hbm(token_table), tokens_c)


def score_kernel(factor, arrays, chunks, merge, relay, base_ref, *refs):
    cut = iter(refs)
    take = lambda n: [next(cut) for _ in range(n)]
    q_refs, c_refs, old_refs, relayed, (out_ref,), halves = (
        take(n) for n in (arrays, len(chunks), merge, 2 * relay, 1, 2 * relay))
    if relay:
        rbuf, rsem = take(2)
        arrive = [vm_copy(relayed[h].at[pl.ds(4 * h, 4)], rbuf.at[h], rsem, h) for h in range(2)]
        leave = [vm_copy(rbuf.at[h], halves[h], rsem, 2 + h) for h in range(2)]
        for copy in arrive:
            copy.start()
    lane = lax.broadcasted_iota(jnp.int32, (1, 128), 1)
    k2 = factor * math.log2(math.e)
    places = [(ref, p) for ref in q_refs for p in range(0, ref.shape[0], 4)]
    rows = 8 * OWN
    for tile in range(len(places) // 2):
        pair = places[2 * tile:2 * tile + 2]
        if pair[0][0] is pair[1][0]:
            q = pair[0][0][:, 0:OWN, :].reshape(rows, WIDTH)
        else:
            q = jnp.concatenate([ref[p:p + 4, 0:OWN, :].reshape(4 * OWN, WIDTH) for ref, p in pair], axis=0)
        wanted = []
        for ref, first in pair:
            for p in range(first, first + 4):
                found = ref[p, OWN:PIECE, 0:384].astype(F32)[0:1, :]
                row = found[:, 0:128] * 65536.0 + found[:, 128:256] * 256.0 + found[:, 256:384]
                wanted.append(jnp.broadcast_to(row, (OWN, OWN)).T.astype(jnp.int32))
        wanted = jnp.concatenate(wanted, axis=0)
        high = jnp.full((rows, 128), -jnp.inf, F32)
        total = jnp.zeros((rows, 128), F32)
        picked = jnp.zeros((rows, 128), F32)
        for k in range(2 * len(chunks)):
            j = chunks[k // 2] + k % 2
            c = c_refs[k // 2][k % 2 * CHUNK:k % 2 * CHUNK + CHUNK, :]
            sc = lax.dot_general(q, c, (((1,), (1,)), ((), ())), preferred_element_type=F32)
            groups = [sc[:, i * 128:(i + 1) * 128] for i in range(CHUNK // 128)]
            new_high = jnp.maximum(high, functools.reduce(jnp.maximum, groups))
            fresh = functools.reduce(jnp.add, [jnp.exp2((g - new_high) * k2) for g in groups])
            total = fresh if k == 0 else total * jnp.exp2((high - new_high) * k2) + fresh
            high = new_high
            for i, g in enumerate(groups):
                picked = jnp.where(wanted == lane + (base_ref[2 * j + i // 2] + i % 2 * 128), g, picked)
        if relay and tile == 0:
            for one, two in zip(arrive, leave):
                one.wait()
                two.start()
        for k in range(8):
            p = 8 * tile + k
            at = slice(k * OWN, (k + 1) * OWN)
            by_lane = high[at].T
            top = jnp.max(by_lane, axis=0, keepdims=True)
            summed = jnp.sum(total[at].T * jnp.exp2((by_lane - top) * k2), axis=0, keepdims=True)
            lse = top * factor + jnp.log(summed)
            score = jnp.sum(picked[at].T, axis=0, keepdims=True) * factor
            if merge:
                old = old_refs[0][p, 0:1, :]
                above = jnp.maximum(old, lse)
                lse = above + jnp.log(jnp.exp(old - above) + jnp.exp(lse - above))
                score += old_refs[0][p, 1:2, :]
            out_ref[p, 0:1, :] = lse
            out_ref[p, 1:2, :] = score
    if relay:
        for copy in leave:
            copy.wait()


def block_stats(factor, bases, queries, candidates, old=None, relay=()):
    pieces = sum(q.shape[0] for q in queries)
    merge = [] if old is None else [old]
    scratch = []
    shapes, specs = [jax.ShapeDtypeStruct((pieces, 2, OWN), F32)], [VMEM]
    if relay:
        half = (4, PIECE, WIDTH)
        shapes += [pltpu.HBM(half, BF)] * 2
        specs += [ANY] * 2
        scratch += [pltpu.VMEM((2,) + half, BF), pltpu.SemaphoreType.DMA((4,))]
    result = pl.pallas_call(
        functools.partial(
            score_kernel, factor, len(queries), tuple(j for _, j in candidates), len(merge), len(relay) // 2),
        in_specs=[SMEM] + [VMEM] * (len(queries) + len(candidates) + len(merge)) + [ANY] * len(relay),
        out_specs=specs,
        out_shape=shapes,
        scratch_shapes=scratch,
        compiler_params=pltpu.CompilerParams(vmem_limit_bytes=32 << 20),
        cost_estimate=SMALL,
        name="scores",
    )(bases, *[q if q.shape[0] == 4 else in_hbm(q)[0] for q in queries], *in_hbm(*[array for array, _ in candidates]), *merge,
      *in_hbm(*relay))
    return result if relay else result[0]


def after(value, *earlier):
    return lax.optimization_barrier((value,) + earlier)[0]


def per_device(doc_states, phrase_start, phrase_span, start_in, start_out, end_in, end_out, token_table, queries, targets):
    factor = 3.0 / math.sqrt(WIDTH)
    dp = lax.axis_index("dp")
    mp = lax.axis_index("mp")
    core = dp % 2
    device = dp * 2 + mp

    core_ref = core.reshape(1)
    own, pay1, pay2 = pack(core_ref, targets, queries, token_table, start_in, start_out, end_in, end_out)
    from_z = send(own, class_partner)
    tokens_c = send(token_table, other_core)
    mine2 = send(pay2, class_partner)
    mine1 = send(pay1, mp_partner)

    base = jnp.concatenate([own, after(from_z, tokens_c)], axis=0)
    left = send(base, along(True, 1))
    right = send(base, along(True, -1))
    far = send(base, along(True, 2))

    ends = jnp.minimum(phrase_start + phrase_span, doc_states.shape[0] - 1)
    index = jnp.concatenate([phrase_start, ends])
    rows = jnp.take(doc_states, after(index, base), axis=0, mode="clip")

    part = join([base, after(left, rows), right, far])
    up = send(part, along(False, 1))
    down = send(part, along(False, -1))

    mine1, mine2 = after(mine1, part), after(mine2, part)
    theirs1 = send(mine1, other_core)
    theirs2 = send(mine2, other_core)
    phrases, tokens = make_phrases(
        core_ref, rows, start_in, start_out, end_in, end_out, mine1, mine2, theirs1, theirs2, token_table, tokens_c
    )
    phrases_c = send(phrases, other_core)

    quarters = jnp.arange(4, dtype=jnp.int32) * 256
    bases = jnp.concatenate([
        PHRASES + (device ^ jnp.array([0, 2, 1, 3], jnp.int32)) * 256, dp * 1024 + quarters, (dp ^ 1) * 1024 + quarters
    ]).astype(jnp.int32)
    here = [(phrases, 2), (tokens, 0)]
    score = functools.partial(block_stats, factor, bases)
    early = score([part], here)
    there = [(after(phrases_c, early), 4)]
    stats1, half1, half2 = score([part], there, old=early, relay=(up, down))
    far1 = send(half1, along(False, 1))
    far2 = send(half2, along(False, -1))
    up, down = after(up, stats1), after(down, stats1)
    stats2 = score([up, down], here + there)
    stats3 = score([after(far1, stats2), far2], here + there)
    stats = jnp.concatenate([stats1, stats2, stats3], axis=0)

    y, x, zh = dp // 16, dp // 4 % 4, dp // 2 % 2
    n = jnp.arange(32, dtype=jnp.int32)
    dy, dx, s = (n // 8 - y) % 4, (n // 2 - x) % 4, (n % 2) ^ zh
    i = jnp.where(core == 0, dx, dy)
    j = jnp.where(core == 0, dy, dx)
    first = jnp.where(i == 3, 1, jnp.where(i == 1, 2, jnp.where(i == 2, 3, 0)))
    block = jnp.where(j == 0, 0, jnp.where(j == 3, 1, jnp.where(j == 1, 2, 3)))
    place = block * 8 + first * 2 + s
    ordered = jnp.take(stats, place, axis=0, mode="clip")
    received = lax.all_to_all(
        ordered, AXES, split_axis=0, concat_axis=0, tiled=True, axis_index_groups=owner_groups()
    )
    lse, score = received[:, 0, :], received[:, 1, :]
    top = jnp.max(lse, axis=0)
    return top + jnp.log(jnp.sum(jnp.exp(lse - top[None, :]), axis=0)) - jnp.sum(score, axis=0)


def solution(mesh):
    in_specs = (
        P("dp", None),
        P("dp"),
        P("dp"),
        P(None, "mp"),
        P("mp", None),
        P(None, "mp"),
        P("mp", None),
        P(("dp", "mp"), None),
        P(("dp", "mp"), None),
        P(("dp", "mp")),
    )
    return jax.shard_map(
        per_device, mesh=mesh, in_specs=in_specs, out_specs=P(("dp", "mp")), check_vma=False
    )
```

```python
import functools
import math

import jax
import jax.numpy as jnp
from jax import lax
from jax.experimental import pallas as pl
from jax.experimental.pallas import tpu as pltpu
from jax.sharding import PartitionSpec as P

BF = jnp.bfloat16
F32 = jnp.float32
AXES = ("dp", "mp")
NY, NX = 4, 4
DEVICES = 128
OWN = 128
SLAB = 8
PIECE = OWN + SLAB
WIDTH = 1024
HALF = 512
PHRASES = 65536
CHUNK = 512
TILES = 4
GELU = math.sqrt(2 / math.pi)


def coords(n):
    return n // 32, n // 8 % 4, n // 4 % 2, n // 2 % 2, n % 2


def linear(y, x, zh, c, zl):
    return (((y % NY) * NX + x % NX) * 2 + zh) * 4 + c * 2 + zl


def pairs(move):
    return [(n, linear(*move(*coords(n)))) for n in range(DEVICES)]


def send(value, move):
    return lax.ppermute(value, AXES, pairs(move))


def along(first, step):
    def move(y, x, zh, c, zl):
        if (c == 0) == first:
            return y, x + step, zh, c, zl
        return y + step, x, zh, c, zl

    return move


def other_core(y, x, zh, c, zl):
    return y, x, zh, 1 - c, zl


def mp_partner(y, x, zh, c, zl):
    return y, x, zh, c, 1 - zl


def class_partner(y, x, zh, c, zl):
    return y, x, 1 - zh, c, 1 - zl


def owner_groups():
    return [
        [linear(y, x, zh, c, zh ^ k) for y in range(NY) for x in range(NX) for zh in range(2)]
        for c in range(2)
        for k in range(2)
    ]


def vm_copy(src, dst, sems, k):
    return pltpu.make_async_copy(src, dst, sems.at[k])


ANY = pl.BlockSpec(memory_space=pl.ANY)
SMEM = pl.BlockSpec(memory_space=pltpu.SMEM)
VMEM = pl.BlockSpec(memory_space=pltpu.VMEM)
SMALL = pl.CostEstimate(flops=1 << 20, bytes_accessed=1 << 16, transcendentals=0)


def in_hbm(*arrays):
    return [pltpu.with_memory_space_constraint(array, pltpu.HBM) for array in arrays]


ROWS_ONE, ROWS_TWO = 1152, 896


def pack_kernel(core_ref, tgt_ref, q_ref, tok_ref, si_ref, so_ref, ei_ref, eo_ref, own_ref, one_ref, two_ref, one, two, sems):
    queries = vm_copy(q_ref, own_ref.at[0, pl.ds(0, OWN), :], sems, 9)
    queries.start()
    at = pl.multiple_of(core_ref[0] * 512, 512)
    small = pl.ds(pl.multiple_of(core_ref[0] * 256, 256), 256)
    loads = [
        vm_copy(src, dst, sems, k)
        for k, (src, dst) in enumerate((
            (si_ref.at[pl.ds(at + 128, 384), :], two.at[pl.ds(0, 384), :]),
            (ei_ref.at[pl.ds(at, 512), :], two.at[pl.ds(384, 512), :]),
            (tok_ref.at[:, pl.ds(0, 512)], one.at[pl.ds(0, 256), :]),
            (tok_ref.at[:, pl.ds(512, 512)], one.at[pl.ds(256, 256), :]),
            (so_ref.at[small, :], one.at[pl.ds(512, 256), :]),
            (eo_ref.at[small, :], one.at[pl.ds(768, 256), :]),
            (si_ref.at[pl.ds(at, 128), :], one.at[pl.ds(1024, 128), :]),
        ))
    ]
    for load in loads:
        load.start()
    target = tgt_ref[...]
    digits = [jnp.right_shift(target, 16), jnp.bitwise_and(jnp.right_shift(target, 8), 255), jnp.bitwise_and(target, 255)]
    row = jnp.concatenate(digits + [jnp.zeros((1, WIDTH - 3 * OWN), jnp.int32)], axis=1).astype(F32)
    own_ref[0, OWN:PIECE, :] = jnp.broadcast_to(row, (SLAB, WIDTH)).astype(BF)
    stores = [vm_copy(two, two_ref, sems, 7), vm_copy(one, one_ref, sems, 8)]
    for load in loads[:2]:
        load.wait()
    stores[0].start()
    for load in loads[2:]:
        load.wait()
    stores[1].start()
    for store in stores:
        store.wait()
    queries.wait()


def pack(core, targets, queries, tokens, si, so, ei, eo):
    return pl.pallas_call(
        pack_kernel,
        in_specs=[SMEM, VMEM] + [ANY] * 6,
        out_specs=[VMEM, ANY, ANY],
        out_shape=[jax.ShapeDtypeStruct((1, PIECE, WIDTH), BF)]
        + [jax.ShapeDtypeStruct((n, 512), BF) for n in (ROWS_ONE, ROWS_TWO)],
        scratch_shapes=[pltpu.VMEM((n, 512), BF) for n in (ROWS_ONE, ROWS_TWO)] + [pltpu.SemaphoreType.DMA((10,))],
        compiler_params=pltpu.CompilerParams(vmem_limit_bytes=8 << 20),
        cost_estimate=SMALL,
        name="pack",
    )(core, targets.reshape(1, OWN), *in_hbm(queries, tokens, si, so, ei, eo))


def join_kernel(spans, *refs):
    ins, out, sems = refs[:len(spans)], refs[-2], refs[-1]
    loads, at = [], 0
    for k, (first, n) in enumerate(spans):
        loads.append(vm_copy(ins[k].at[pl.ds(first, n)], out.at[pl.ds(at, n)], sems, k))
        at += n
    for load in loads:
        load.start()
    for load in loads:
        load.wait()


def join(parts, spans=None):
    spans = spans or [(0, part.shape[0]) for part in parts]
    shape = (sum(n for _, n in spans),) + parts[0].shape[1:]
    return pl.pallas_call(
        functools.partial(join_kernel, tuple(spans)),
        in_specs=[ANY] * len(parts),
        out_specs=VMEM,
        out_shape=jax.ShapeDtypeStruct(shape, parts[0].dtype),
        scratch_shapes=[pltpu.SemaphoreType.DMA((len(parts),))],
        compiler_params=pltpu.CompilerParams(vmem_limit_bytes=8 << 20),
        cost_estimate=SMALL,
        name="join",
    )(*in_hbm(*parts))


def phrase_kernel(core_ref, rows_ref, si_ref, so_ref, ei_ref, eo_ref, m1_ref, m2_ref, t1_ref, t2_ref, tok_ref, tokc_ref,
                  out_ref, tokens_ref, rows, w_in, w_out, tokens, sems):
    n = rows_ref.shape[0] // 2
    core = core_ref[0]
    mine, others = pl.ds(0, 512), pl.ds(512, 512)
    groups = [
        [
            (rows_ref.at[pl.ds(half * n, n), :], rows.at[pl.ds(half * n, n), :]),
            (first, w_in.at[half, :, mine]),
            (second, w_out.at[half, mine, :]),
        ]
        for half, (first, second) in enumerate(((si_ref, so_ref), (ei_ref, eo_ref)))
    ]
    for c, one, two in ((core, m1_ref, m2_ref), (1 - core, t1_ref, t2_ref)):
        at = pl.multiple_of(c * 512, 512)
        small = pl.ds(pl.multiple_of(512 + c * 256, 256), 256)
        groups[0] += [
            (one.at[pl.ds(512, 256), :], w_out.at[0, small, :]),
            (one.at[pl.ds(1024, 128), :], w_in.at[0, pl.ds(at, 128), others]),
            (two.at[pl.ds(0, 384), :], w_in.at[0, pl.ds(at + 128, 384), others]),
        ]
        groups[1] += [
            (one.at[pl.ds(768, 256), :], w_out.at[1, small, :]),
            (two.at[pl.ds(384, 512), :], w_in.at[1, pl.ds(at, 512), others]),
        ]
    groups.append([(tok_ref, tokens.at[pl.ds(0, 256), :]), (tokc_ref, tokens.at[pl.ds(256, 256), :])] + [
        (one.at[pl.ds(h * 256, 256), :], tokens.at[pl.ds(512 + 256 * k, 256), pl.ds(h * 512, 512)])
        for k, one in enumerate((m1_ref, t1_ref)) for h in range(2)
    ])
    copies, k = [], 0
    for group in groups:
        copies.append([vm_copy(src, dst, sems, k + i) for i, (src, dst) in enumerate(group)])
        k += len(group)
    for group in copies:
        for copy in group:
            copy.start()

    for half in range(2):
        for copy in copies[half]:
            copy.wait()
        if half:
            for copy in copies[2]:
                copy.wait()
            stored = vm_copy(tokens, tokens_ref, sems, k)
            stored.start()
        for r in range(TILES):
            at = slice(half * n + r * n // TILES, half * n + (r + 1) * n // TILES)
            x = jnp.dot(rows[at, :], w_in[half], preferred_element_type=F32)
            u = x * (GELU + GELU * 0.044715 * (x * x))
            h = 0.5 * x
            hidden = (h + h * jnp.tanh(u)).astype(BF)
            total = jnp.dot(hidden, w_out[half], preferred_element_type=F32)
            out_ref[r * n // TILES:(r + 1) * n // TILES, half * HALF:(half + 1) * HALF] = total.astype(BF)
    stored.wait()


def make_phrases(core, rows, si, so, ei, eo, mine1, mine2, theirs1, theirs2, token_table, tokens_c):
    n = rows.shape[0] // 2
    tokens = (4 * token_table.shape[0], WIDTH)
    return pl.pallas_call(
        phrase_kernel,
        in_specs=[SMEM] + [ANY] * 11,
        out_specs=[VMEM, ANY],
        out_shape=[jax.ShapeDtypeStruct((n, WIDTH), BF), pltpu.HBM(tokens, BF)],
        scratch_shapes=[
            pltpu.VMEM((2 * n, WIDTH), BF),
            pltpu.VMEM((2, WIDTH, 1024), BF),
            pltpu.VMEM((2, 1024, HALF), BF),
            pltpu.VMEM(tokens, BF),
            pltpu.SemaphoreType.DMA((23,)),
        ],
        compiler_params=pltpu.CompilerParams(vmem_limit_bytes=24 << 20),
        cost_estimate=SMALL,
        name="phrases",
    )(core, *in_hbm(rows, si, so, ei, eo), mine1, *in_hbm(mine2), theirs1, theirs2, *in_hbm(token_table), tokens_c)


def score_kernel(factor, arrays, chunks, merge, base_ref, *refs):
    q_refs, c_refs, refs = refs[:arrays], refs[arrays:arrays + len(chunks)], refs[arrays + len(chunks):]
    old_refs, out_ref = refs[:merge], refs[merge]
    lane = lax.broadcasted_iota(jnp.int32, (1, 128), 1)
    k2 = factor * math.log2(math.e)
    places = [(ref, p) for ref in q_refs for p in range(0, ref.shape[0], 4)]
    rows = 8 * OWN
    for tile in range(len(places) // 2):
        pair = places[2 * tile:2 * tile + 2]
        if pair[0][0] is pair[1][0]:
            q = pair[0][0][:, 0:OWN, :].reshape(rows, WIDTH)
        else:
            q = jnp.concatenate([ref[p:p + 4, 0:OWN, :].reshape(4 * OWN, WIDTH) for ref, p in pair], axis=0)
        wanted = []
        for ref, first in pair:
            for p in range(first, first + 4):
                found = ref[p, OWN:PIECE, 0:384].astype(F32)[0:1, :]
                row = found[:, 0:128] * 65536.0 + found[:, 128:256] * 256.0 + found[:, 256:384]
                wanted.append(jnp.broadcast_to(row, (OWN, OWN)).T.astype(jnp.int32))
        wanted = jnp.concatenate(wanted, axis=0)
        high = jnp.full((rows, 128), -jnp.inf, F32)
        total = jnp.zeros((rows, 128), F32)
        picked = jnp.zeros((rows, 128), F32)
        for k in range(2 * len(chunks)):
            j = chunks[k // 2] + k % 2
            c = c_refs[k // 2][k % 2 * CHUNK:k % 2 * CHUNK + CHUNK, :]
            sc = lax.dot_general(q, c, (((1,), (1,)), ((), ())), preferred_element_type=F32)
            groups = [sc[:, i * 128:(i + 1) * 128] for i in range(CHUNK // 128)]
            new_high = jnp.maximum(high, functools.reduce(jnp.maximum, groups))
            fresh = functools.reduce(jnp.add, [jnp.exp2((g - new_high) * k2) for g in groups])
            total = fresh if k == 0 else total * jnp.exp2((high - new_high) * k2) + fresh
            high = new_high
            for i, g in enumerate(groups):
                picked = jnp.where(wanted == lane + (base_ref[2 * j + i // 2] + i % 2 * 128), g, picked)
        for k in range(8):
            p = 8 * tile + k
            at = slice(k * OWN, (k + 1) * OWN)
            by_lane = high[at].T
            top = jnp.max(by_lane, axis=0, keepdims=True)
            summed = jnp.sum(total[at].T * jnp.exp2((by_lane - top) * k2), axis=0, keepdims=True)
            lse = top * factor + jnp.log(summed)
            score = jnp.sum(picked[at].T, axis=0, keepdims=True) * factor
            if merge:
                old = old_refs[0][p, 0:1, :]
                above = jnp.maximum(old, lse)
                lse = above + jnp.log(jnp.exp(old - above) + jnp.exp(lse - above))
                score += old_refs[0][p, 1:2, :]
            out_ref[p, 0:1, :] = lse
            out_ref[p, 1:2, :] = score


def block_stats(factor, bases, queries, candidates, old=None):
    pieces = sum(q.shape[0] for q in queries)
    merge = [] if old is None else [old]
    return pl.pallas_call(
        functools.partial(score_kernel, factor, len(queries), tuple(j for _, j in candidates), len(merge)),
        in_specs=[SMEM] + [VMEM] * (len(queries) + len(candidates) + len(merge)),
        out_specs=VMEM,
        out_shape=jax.ShapeDtypeStruct((pieces, 2, OWN), F32),
        compiler_params=pltpu.CompilerParams(vmem_limit_bytes=32 << 20),
        cost_estimate=SMALL,
        name="scores",
    )(bases, *[q if q.shape[0] == 4 else in_hbm(q)[0] for q in queries], *in_hbm(*[array for array, _ in candidates]), *merge)


def halves_kernel(up_ref, down_ref, one_ref, two_ref, sems):
    copies = [vm_copy(up_ref.at[pl.ds(0, 4)], one_ref, sems, 0), vm_copy(down_ref.at[pl.ds(4, 4)], two_ref, sems, 1)]
    for copy in copies:
        copy.start()
    for copy in copies:
        copy.wait()


def halves(up, down):
    return pl.pallas_call(
        halves_kernel,
        in_specs=[ANY] * 2,
        out_specs=[VMEM] * 2,
        out_shape=[jax.ShapeDtypeStruct((4, PIECE, WIDTH), BF)] * 2,
        scratch_shapes=[pltpu.SemaphoreType.DMA((2,))],
        compiler_params=pltpu.CompilerParams(vmem_limit_bytes=8 << 20),
        cost_estimate=SMALL,
        name="halves",
    )(*in_hbm(up, down))


def after(value, *earlier):
    return lax.optimization_barrier((value,) + earlier)[0]


def per_device(doc_states, phrase_start, phrase_span, start_in, start_out, end_in, end_out, token_table, queries, targets):
    factor = 3.0 / math.sqrt(WIDTH)
    dp = lax.axis_index("dp")
    mp = lax.axis_index("mp")
    core = dp % 2
    device = dp * 2 + mp

    core_ref = core.reshape(1)
    own, pay1, pay2 = pack(core_ref, targets, queries, token_table, start_in, start_out, end_in, end_out)
    from_z = send(own, class_partner)
    tokens_c = send(token_table, other_core)
    mine2 = send(pay2, class_partner)
    mine1 = send(pay1, mp_partner)

    base = jnp.concatenate([own, after(from_z, tokens_c)], axis=0)
    left = send(base, along(True, 1))
    right = send(base, along(True, -1))
    far = send(base, along(True, 2))

    ends = jnp.minimum(phrase_start + phrase_span, doc_states.shape[0] - 1)
    index = jnp.concatenate([phrase_start, ends])
    rows = jnp.take(doc_states, after(index, base), axis=0, mode="clip")

    part = join([base, after(left, rows), right, far])
    up = send(part, along(False, 1))
    down = send(part, along(False, -1))

    mine1, mine2 = after(mine1, part), after(mine2, part)
    theirs1 = send(mine1, other_core)
    theirs2 = send(mine2, other_core)
    phrases, tokens = make_phrases(
        core_ref, rows, start_in, start_out, end_in, end_out, mine1, mine2, theirs1, theirs2, token_table, tokens_c
    )
    phrases_c = send(phrases, other_core)

    quarters = jnp.arange(4, dtype=jnp.int32) * 256
    bases = jnp.concatenate([
        PHRASES + (device ^ jnp.array([0, 2, 1, 3], jnp.int32)) * 256, dp * 1024 + quarters, (dp ^ 1) * 1024 + quarters
    ]).astype(jnp.int32)
    here = [(phrases, 2), (tokens, 0)]
    score = functools.partial(block_stats, factor, bases)
    early = score([part], here)
    there = [(after(phrases_c, early), 4)]
    stats1 = score([part], there, old=early)
    up, down = after(up, stats1), after(down, stats1)
    half1, half2 = halves(up, down)
    far1 = send(half1, along(False, 1))
    far2 = send(half2, along(False, -1))
    stats2 = score([up, down], here + there)
    stats3 = score([after(far1, stats2), far2], here + there)
    stats = jnp.concatenate([stats1, stats2, stats3], axis=0)

    y, x, zh = dp // 16, dp // 4 % 4, dp // 2 % 2
    n = jnp.arange(32, dtype=jnp.int32)
    dy, dx, s = (n // 8 - y) % 4, (n // 2 - x) % 4, (n % 2) ^ zh
    i = jnp.where(core == 0, dx, dy)
    j = jnp.where(core == 0, dy, dx)
    first = jnp.where(i == 3, 1, jnp.where(i == 1, 2, jnp.where(i == 2, 3, 0)))
    block = jnp.where(j == 0, 0, jnp.where(j == 3, 1, jnp.where(j == 1, 2, 3)))
    place = block * 8 + first * 2 + s
    ordered = jnp.take(stats, place, axis=0, mode="clip")
    received = lax.all_to_all(
        ordered, AXES, split_axis=0, concat_axis=0, tiled=True, axis_index_groups=owner_groups()
    )
    lse, score = received[:, 0, :], received[:, 1, :]
    top = jnp.max(lse, axis=0)
    return top + jnp.log(jnp.sum(jnp.exp(lse - top[None, :]), axis=0)) - jnp.sum(score, axis=0)


def solution(mesh):
    in_specs = (
        P("dp", None),
        P("dp"),
        P("dp"),
        P(None, "mp"),
        P("mp", None),
        P(None, "mp"),
        P("mp", None),
        P(("dp", "mp"), None),
        P(("dp", "mp"), None),
        P(("dp", "mp")),
    )
    return jax.shard_map(
        per_device, mesh=mesh, in_specs=in_specs, out_specs=P(("dp", "mp")), check_vma=False
    )
```
